32 devices in a mesh: band: 2 (over x), tm: 2 (over core), inp: 8 (over z, y).
Axes of the slice: x: 2, y: 2, z: 4, core: 2. Of those that a mesh axis runs over, the one named last changes fastest.
Arguments:
- samples: int32 [1024, 131072], P('inp', ('band', 'tm')), parts along dimension 1, may hold values from -128 to 127
- flags: int32 [2048], P(('band', 'inp')), parts along dimension 0, may hold values 0 or 1
Outputs:
- visibilities: bfloat16 [256, 2, 1024, 1024], P(('band', 'inp'), None, None, 'tm'), parts along dimension 0
The draws below stay inside these ranges and needn't reach their ends.
There are 2 independent parts, one for each index of `band`. The reference program is written for one: setup_inputs(seed, part) draws one part's arguments, and reference() takes and returns one part's arrays. A program takes and returns all parts, laid end to end along the dimension named above; each array names one. Nothing has to cross between parts.
Inputs may be any that keep to these rules, and one draw needn't show every extreme that they name: `samples`: whole numbers.
All inputs are finite; a program needn't handle non-finite values. No bound on the sum of `flags` on one device may be relied on, other than what follows from the above.
Results may differ from the reference program's by a relative error of at most 0.0056.
Values may be sent and summed in bfloat16 or wider, within the bound.
No kernel may reach another device: no remote copies, remote signals or barrier semaphores. Data moves between devices by JAX's collectives and lax.ppermute only.
A program may use at most 128 MiB of HBM per device.

```python
import math
import jax
import jax.numpy as jnp
from jax import lax

NIN = 1024
NFFT = 1024
TAPS = 4
CH_FIRST = 384
CH = 128
NFR = 64
NT = 65536


def set_ends(entries, rng, smallest, high):
    longest = entries.shape.index(max(entries.shape))
    spots = []
    for shift in (0, 1):
        where = [jax.random.randint(jax.random.fold_in(rng, axis), (), 0, length) for axis, length in enumerate(entries.shape)]
        where[longest] = (where[longest] + shift) % entries.shape[longest]
        spots.append(tuple(where))
    return entries.at[spots[0]].set(smallest).at[spots[1]].set(high)


def setup_inputs(seed: int = 0, part: int = 0) -> dict:
    arg_keys = jax.random.split(jax.random.key(seed), 3)
    part_keys = jax.random.split(jax.random.fold_in(arg_keys[2], part), 3)
    samples = set_ends(jax.random.randint(part_keys[0], (NIN, NT), -128, 128), jax.random.fold_in(part_keys[0], 1), -128, 127).astype(jnp.int32)
    flags = set_ends((jax.random.randint(part_keys[1], (NIN,), 0, 8) < 7).astype(jnp.int32), jax.random.fold_in(part_keys[1], 1), 0, 1)
    return dict(samples=samples, flags=flags)


def window_table():
    positions = jnp.arange(TAPS * NFFT, dtype=jnp.float32) + 0.5
    shaped = jnp.sinc((positions - TAPS * NFFT / 2) / NFFT)
    taper = 0.5 - 0.5 * jnp.cos(2 * math.pi * positions / (TAPS * NFFT))
    return (shaped * taper).reshape(TAPS, NFFT)

def transform_table():
    sample_idx = jnp.arange(NFFT, dtype=jnp.int32)
    chan_idx = CH_FIRST + jnp.arange(CH, dtype=jnp.int32)
    angles = (sample_idx[:, None] * chan_idx[None, :] % NFFT).astype(jnp.float32) * (2 * math.pi / NFFT)
    both = jnp.stack([jnp.cos(angles), -jnp.sin(angles)], axis=1) / math.sqrt(NFFT)
    return both.reshape(NFFT, 2 * CH)

def filter_bank(extended, window, frames):
    summed = jnp.zeros((extended.shape[0], frames, NFFT), jnp.float32)
    for tap_index in range(TAPS):
        begin = TAPS - 1 - tap_index
        summed = summed + window[tap_index] * extended[:, begin:begin + frames]
    return summed

def transform(filtered, table):
    rows, frames, width = filtered.shape
    out = jnp.dot(filtered.reshape(rows * frames, width), table, precision=lax.Precision.HIGHEST, preferred_element_type=jnp.float32)
    return out.reshape(rows, frames, 2, CH)

def correlate_single(block):
    left_side = block.astype(jnp.float32)
    depth = 2 * left_side.shape[0]
    real_rows = left_side.reshape(depth, NIN)
    imag_rows = jnp.stack([left_side[:, 1], -left_side[:, 0]], axis=1).reshape(depth, NIN)
    left_both = jnp.stack([real_rows, imag_rows])
    out = jnp.einsum('rka,kb->rab', left_both, real_rows, precision=lax.Precision.HIGHEST)
    return out.astype(jnp.bfloat16)

def reference(samples, flags):
    voltage = (samples.astype(jnp.float32) / 128.0).astype(jnp.bfloat16)
    values = voltage.astype(jnp.float32).reshape(NIN, NFR, NFFT)
    leading = jnp.zeros((NIN, TAPS - 1, NFFT), jnp.float32)
    extended = jnp.concatenate([leading, values], axis=1)
    filtered = filter_bank(extended, window_table(), NFR)
    spectra = transform(filtered, transform_table())
    weight = flags.astype(jnp.float32)[:, None, None, None]
    channels = (spectra * weight).astype(jnp.bfloat16).transpose(3, 1, 2, 0)
    return lax.map(correlate_single, channels)
```

```python
import functools
import math

import jax
import jax.numpy as jnp
import ml_dtypes
import numpy as np
from jax import lax
from jax.experimental import pallas as pl
from jax.experimental.pallas import tpu as pltpu
from jax.sharding import PartitionSpec as P

NFFT = 1024
TAPS = 4
CH_FIRST = 384
CH = 128
LANES = 128
STEP = 4
HALF = 16
VMEM = 56 * 2**20


def window_values():
    positions = np.arange(TAPS * NFFT, dtype=np.float64) + 0.5
    shaped = np.sinc((positions - TAPS * NFFT / 2) / NFFT)
    taper = 0.5 - 0.5 * np.cos(2 * math.pi * positions / (TAPS * NFFT))
    return (shaped * taper).reshape(TAPS, NFFT)


def transform_values():
    sample_idx = np.arange(NFFT)
    chan_idx = CH_FIRST + np.arange(CH)
    angles = (sample_idx[:, None] * chan_idx[None, :] % NFFT) * (2 * math.pi / NFFT)
    both = np.concatenate([np.cos(angles), -np.sin(angles)], axis=1)
    return both / math.sqrt(NFFT)


def split_table():
    table = transform_values()
    high = table.astype(ml_dtypes.bfloat16)
    low = (table - high.astype(np.float64)).astype(ml_dtypes.bfloat16)
    return high, low


def ring(length, by):
    return [(i, (i + by) % length) for i in range(length)]


def channelize_kernel(n, cuts, me_ref, flags_ref, window_ref, high_ref, low_ref, prev_ref,
                      samples_ref, *rest):
    outs, (carry, filt_high, filt_low, spectra) = rest[:-4], rest[-4:]
    step = pl.program_id(0)
    rows = samples_ref.shape[0]

    @pl.when(step == 0)
    def _():
        carry[...] = prev_ref[:, NFFT:].astype(jnp.float32)

    width = 256
    for lane in range(0, NFFT, width):
        taps = [window_ref[k : k + 1, lane : lane + width] for k in range(TAPS)]

        def strip(r, _):
            at = pl.ds(pl.multiple_of(r * 16, 16), 16)
            held = [carry[at, j * NFFT + lane : j * NFFT + lane + width] for j in range(TAPS - 1)]
            for f in range(STEP):
                value = samples_ref[at, f * NFFT + lane : f * NFFT + lane + width]
                held.append(value.astype(jnp.float32))
                total = taps[0] * held[-1]
                for k in range(1, TAPS):
                    total = total + taps[k] * held[-1 - k]
                high = total.astype(jnp.bfloat16)
                low = (total - high.astype(jnp.float32)).astype(jnp.bfloat16)
                to = pl.ds(pl.multiple_of(f * rows + r * 16, 16), 16)
                filt_high[to, lane : lane + width] = high
                filt_low[to, lane : lane + width] = low
                held = held[1:]
            for j in range(TAPS - 1):
                carry[at, j * NFFT + lane : j * NFFT + lane + width] = held[j]
            return 0

        lax.fori_loop(0, rows // 16, strip, 0)

    dot = functools.partial(jnp.dot, preferred_element_type=jnp.float32)
    for f in range(STEP):
        at = slice(f * rows, (f + 1) * rows)
        high = filt_high[at, :]
        out = dot(high, high_ref[...]) + dot(filt_low[at, :], high_ref[...]) + dot(high, low_ref[...])
        for p in range(2):
            part = out[:, p * CH : (p + 1) * CH].T * flags_ref[...]
            row = (p * HALF + step * STEP + f) * CH
            spectra[pl.ds(pl.multiple_of(row, CH), CH), :] = part

    @pl.when(step == pl.num_programs(0) - 1)
    def _():
        per = CH // n
        for d in range(n):
            first = lax.rem(me_ref[0] + d, n) * per
            begin = 0
            for g, count in enumerate(cuts):
                for c in range(count):
                    picked = spectra[pl.ds(first + begin + c, 2 * HALF, stride=CH), :]
                    outs[g * n + d][c] = picked.astype(jnp.bfloat16)
                begin += count


def channelize(me, samples, prev, prev_block, first_step, flags, n, cuts):
    rows = samples.shape[0]
    high, low = split_table()
    whole = lambda *shape: pl.BlockSpec(shape, lambda i, me: (0,) * len(shape))
    shapes = [(count, 2 * HALF, rows) for count in cuts for _ in range(n)]
    steps = HALF // STEP
    out = pl.pallas_call(
        functools.partial(channelize_kernel, n, cuts),
        grid_spec=pltpu.PrefetchScalarGridSpec(
            num_scalar_prefetch=1,
            grid=(steps,),
            in_specs=[
                whole(1, rows),
                whole(TAPS, NFFT),
                whole(NFFT, 2 * CH),
                whole(NFFT, 2 * CH),
                pl.BlockSpec((rows, TAPS * NFFT), lambda i, me: (0, prev_block)),
                pl.BlockSpec((rows, STEP * NFFT), lambda i, me: (0, first_step + i)),
            ],
            out_specs=[whole(*shape) for shape in shapes],
            scratch_shapes=[
                pltpu.VMEM((rows, (TAPS - 1) * NFFT), jnp.float32),
                pltpu.VMEM((STEP * rows, NFFT), jnp.bfloat16),
                pltpu.VMEM((STEP * rows, NFFT), jnp.bfloat16),
                pltpu.VMEM((2 * HALF * CH, LANES), jnp.float32),
            ],
        ),
        out_shape=[jax.ShapeDtypeStruct(shape, jnp.bfloat16) for shape in shapes],
        compiler_params=pltpu.CompilerParams(vmem_limit_bytes=VMEM),
        cost_estimate=pl.CostEstimate(
            flops=6 * 2 * rows * HALF * NFFT * 2 * CH,
            bytes_accessed=rows * (HALF + TAPS) * NFFT * 4,
            transcendentals=0,
        ),
        name="channelize",
    )(me, flags, jnp.asarray(window_values() / 128, jnp.float32), jnp.asarray(high),
      jnp.asarray(low), prev, samples)
    return [out[g * n : (g + 1) * n] for g in range(len(cuts))]


def correlate_kernel(n, tiles, place_ref, *rest):
    blocks, (out_ref, left, turned) = rest[:4], rest[-3:]
    me, half = place_ref[0], place_ref[1]
    for d in range(n):
        src = lax.rem(me + (n - d), n)
        for b, block in enumerate(blocks):
            real = block[d, 0, :HALF, :]
            imag = block[d, 0, HALF:, :]
            low = slice(b * HALF, (b + 1) * HALF)
            high = slice((4 + b) * HALF, (5 + b) * HALF)
            left[src, low, :] = real
            left[src, high, :] = imag
            turned[src, low, :] = imag
            turned[src, high, :] = -real
    right = jnp.concatenate([left[half * tiles + j] for j in range(tiles)], axis=1)
    dims = (((0,), (0,)), ((), ()))

    def product(s, _):
        to = pl.ds(pl.multiple_of(s * LANES, LANES), LANES)
        for part, source in enumerate((left, turned)):
            out = lax.dot_general(source[s], right, dims, preferred_element_type=jnp.float32)
            out_ref[0, part, to, :] = out.astype(jnp.bfloat16)
        return 0

    lax.fori_loop(0, n, product, 0)


def correlate(place, blocks, offsets, first, count, per, width, before):
    n = blocks[0].shape[0]
    rows = blocks[0].shape[3]
    in_specs = [
        pl.BlockSpec((n, 1, 2 * HALF, rows), functools.partial(lambda o, i, place: (0, o + i, 0, 0), o))
        for o in offsets
    ]
    operands = list(blocks)
    aliases = {}
    if before is not None:
        in_specs.append(pl.BlockSpec(memory_space=pl.ANY))
        operands.append(before)
        aliases = {1 + 4: 0}
    shape = (per, 2, n * rows, width)
    return pl.pallas_call(
        functools.partial(correlate_kernel, n, width // rows),
        grid_spec=pltpu.PrefetchScalarGridSpec(
            num_scalar_prefetch=1,
            grid=(count,),
            in_specs=in_specs,
            out_specs=pl.BlockSpec((1,) + shape[1:], lambda i, place: (first + i, 0, 0, 0)),
            scratch_shapes=[pltpu.VMEM((n, 8 * HALF, rows), jnp.bfloat16)] * 2,
        ),
        out_shape=jax.ShapeDtypeStruct(shape, jnp.bfloat16),
        input_output_aliases=aliases,
        compiler_params=pltpu.CompilerParams(vmem_limit_bytes=VMEM),
        cost_estimate=pl.CostEstimate(
            flops=count * 2 * 2 * 8 * HALF * n * rows * width,
            bytes_accessed=count * 2 * n * rows * width * 2,
            transcendentals=0,
        ),
        name="correlate",
    )(place, *operands)


def exchanged(parts, order):
    n = len(parts)
    out = list(parts)
    for d in order:
        out[d] = lax.ppermute(parts[d], "inp", ring(n, d))
    return out


def tiled_local(samples, flags):
    n = lax.axis_size("inp")
    tm = lax.axis_size("tm")
    rows = samples.shape[0]
    per = CH // n
    me = lax.axis_index("inp").astype(jnp.int32)
    half = lax.axis_index("tm").astype(jnp.int32)
    weight = flags.astype(jnp.float32).reshape(1, rows)
    order = sorted(range(1, n), key=lambda d: abs(d - n / 2))
    cuts = (per - 6, 6)
    place = jnp.stack([me, half])

    (late,) = channelize(me.reshape(1), samples, samples, HALF // STEP - 1, HALF // STEP, weight, n, (per,))
    late_in = exchanged(late, order)
    tail = samples[:, samples.shape[1] - TAPS * NFFT :].astype(jnp.bfloat16)
    halo = lax.ppermute(tail, "tm", [(i, i + 1) for i in range(tm - 1)])
    early = channelize(me.reshape(1), samples, halo, 0, 0, weight, n, cuts)
    swap = [(i, tm - 1 - i) for i in range(tm)]
    late_own = jnp.stack(late_in)
    late_other = lax.ppermute(late_own, "tm", swap)
    result, first = None, 0
    for part, count in zip(early, cuts):
        own = jnp.stack(exchanged(part, order))
        other = lax.ppermute(own, "tm", swap)
        result = correlate(place, (late_own, late_other, own, other), (first, first, 0, 0), first,
                           count, per, n * rows // tm, result)
        first += count
    return result


def filter_bank(extended, window, frames):
    return sum(
        window[k] * extended[:, TAPS - 1 - k : TAPS - 1 - k + frames] for k in range(TAPS)
    )


def plain_local(samples, flags):
    rows = samples.shape[0]
    frames = samples.shape[1] // NFFT
    window = jnp.asarray(window_values(), jnp.float32)
    table = jnp.asarray(transform_values(), jnp.float32)
    voltage = (samples.astype(jnp.float32) / 128.0).reshape(rows, frames, NFFT)
    length = lax.axis_size("tm")
    tail = voltage[:, frames - (TAPS - 1) :].astype(jnp.bfloat16)
    halo = lax.ppermute(tail, "tm", [(i, i + 1) for i in range(length - 1)])
    extended = jnp.concatenate([halo.astype(jnp.float32), voltage], axis=1)
    filtered = filter_bank(extended, window, frames)
    spectra = jnp.dot(
        filtered.reshape(rows * frames, NFFT),
        table,
        precision=lax.Precision.HIGHEST,
        preferred_element_type=jnp.float32,
    ).reshape(rows, frames, 2, CH)
    weight = flags.astype(jnp.float32)[:, None, None, None]
    channels = (spectra * weight).astype(jnp.bfloat16).transpose(3, 1, 2, 0)
    mine = lax.all_to_all(channels, "inp", split_axis=0, concat_axis=3, tiled=True)
    left = lax.all_gather(mine, "tm", axis=1, tiled=True)
    chans, total_frames, _, total = left.shape
    width = total // length
    depth = 2 * total_frames
    turned = jnp.stack([left[:, :, 1], -left[:, :, 0]], axis=2).reshape(chans, depth, total)
    straight = left.reshape(chans, depth, total)
    right = lax.dynamic_slice_in_dim(straight, lax.axis_index("tm") * width, width, 2)
    both = jnp.stack([straight, turned], axis=1)
    out = jnp.einsum("crka,ckb->crab", both, right, preferred_element_type=jnp.float32)
    return out.astype(jnp.bfloat16)


def local(samples, flags):
    n, tm = lax.axis_size("inp"), lax.axis_size("tm")
    rows, frames = samples.shape[0], samples.shape[1] // NFFT
    fits = rows == LANES and frames == 2 * HALF and tm == 2 and n % tm == 0 and CH // n > 8
    return tiled_local(samples, flags) if fits else plain_local(samples, flags)


def solution(mesh):
    return jax.shard_map(
        local,
        mesh=mesh,
        in_specs=(P("inp", ("band", "tm")), P(("band", "inp"))),
        out_specs=P(("band", "inp"), None, None, "tm"),
        check_vma=False,
    )
```
